32 devices in a mesh: group: 2 (over y), gx: 4 (over z), gy: 2 (over x), ta: 2 (over core).
Axes of the slice: x: 2, y: 2, z: 4, core: 2. Of those that a mesh axis runs over, the one named last changes fastest.
Arguments:
- velocity: float32 [8, 3, 16, 16, 512], P(('group', 'ta'), None, 'gx', 'gy'), parts along dimension 0, may hold values from -4 to 4
- moved_image: float32 [8, 16, 16, 512], P(('group', 'ta'), 'gx', 'gy'), parts along dimension 0, may hold values from -6 to 6
- residual_weight: float32 [8, 16, 16, 512], P(('group', 'ta'), 'gx', 'gy'), parts along dimension 0, may hold values from -6 to 6
- mark_values: bfloat16 [4096, 3, 512], P(('group', 'gx', 'gy', 'ta')), parts along dimension 0, may hold values from -6 to 6
- mark_brick: int32 [4096, 1], P(('group', 'gx', 'gy', 'ta')), parts along dimension 0, may hold values from 0 to 3; in each aligned block of 128 rows (0 to 127, 128 to 255, ...) at most 64 rows name the same one
- mark_cell: int32 [4096, 1], P(('group', 'gx', 'gy', 'ta')), parts along dimension 0, may hold values from 0 to 31
- band_widths: int32 [3], replicated, may hold values from 3 to 8
Outputs:
- gradient: float32 [8, 3, 16, 16, 512], P(('group', 'ta'), None, 'gx', 'gy'), parts along dimension 0
The draws below stay inside these ranges and needn't reach their ends.
There are 2 independent parts, one for each index of `group`. The reference program is written for one: setup_inputs(seed, part) draws one part's arguments, and reference() takes and returns one part's arrays. A program takes and returns all parts, laid end to end along the dimension named above; an argument that names none is the same for every part. Nothing has to cross between parts.
Inputs may be any that keep to these rules, and one draw needn't show every extreme that they name: `mark_brick`: in the rows of one device no brick index appears more than 64 times.
All inputs are finite; a program needn't handle non-finite values.
Results may differ from the reference program's by a relative error of at most 0.0018.
Values may be sent and summed in bfloat16 or wider, within the bound.
A program may use at most 64 MiB of HBM per device.

```python
import math
import jax
import jax.numpy as jnp
import numpy as np
from jax import lax

CX = 4
CY = 8
NZ = 512
TPTS = 4
BMAX = 8
LM_DEV = 64
NX = 16
NY = 16
LMROWS = 2048
CAP = 64
N_GX = 4
N_GY = 2
N_TA = 2


def place_ends(values, stream_key, smallest, largest):
    longest = values.shape.index(max(values.shape))
    spots = []
    for shift in (0, 1):
        where = [jax.random.randint(jax.random.fold_in(stream_key, axis), (), 0, length) for axis, length in enumerate(values.shape)]
        where[longest] = (where[longest] + shift) % values.shape[longest]
        spots.append(tuple(where))
    return values.at[spots[0]].set(smallest).at[spots[1]].set(largest)


def shard_levels(stream_key, extent, cuts, least, largest):
    gain, own = 1.0, jax.random.fold_in(stream_key, 6)
    for position, shards_of in cuts:
        draws = jnp.exp(jax.random.uniform(jax.random.fold_in(own, position), (shards_of,), jnp.float32, least / len(cuts), largest / len(cuts)))
        gain = gain * jnp.repeat(draws, extent[position] // shards_of).reshape([-1 if axis == position else 1 for axis in range(len(extent))])
    return gain


def shared_out(own_key, own, number, rows, amount, top, most, skew):
    sequence = jax.random.permutation(own_key, amount)
    packed, usual = shares(amount, rows * top, most, skew, True), shares(amount, rows * top, most, skew, False)
    places = jnp.arange(amount)

    def named(lengths, turn):
        used = int((lengths > 0).sum())
        fixed = max(1, used // 4)
        shifted = fixed + (places - fixed + turn * (used - fixed)) % max(1, amount - fixed)
        return jnp.zeros((amount,), jnp.int32).at[sequence[jnp.where(places < fixed, places, shifted)]].set(jnp.asarray(lengths, jnp.int32))

    lengths = jnp.where(number % 4 == 0, named(packed, number // 4), named(usual, number - number // 4 - 1))
    mixed = jax.random.permutation(jax.random.fold_in(own, 3), amount)
    donor, sink = mixed[0:amount // 2 * 2:2], mixed[1:amount // 2 * 2:2]
    margin = jnp.minimum(lengths[donor] - 1, most - lengths[sink]) // 2
    margin = jnp.where((donor == sequence[0]) | (sink == sequence[0]) | (lengths[sink] == 0), 0, jnp.maximum(margin, 0))
    shifted = jax.random.randint(jax.random.fold_in(own, 4), (amount // 2,), 0, 1 << 20) % (margin + 1)
    lengths = lengths.at[donor].add(-shifted).at[sink].add(shifted)
    members = jnp.searchsorted(jnp.cumsum(lengths), jnp.arange(rows * top), side="right").astype(jnp.int32)
    grid = members.reshape(top, rows).T
    grid = grid[jax.random.permutation(jax.random.fold_in(own, 1), rows)]
    turn = jax.random.randint(jax.random.fold_in(own, 2), (rows, 1), 0, top)
    return jnp.take_along_axis(grid, (jnp.arange(top)[None, :] + turn) % top, axis=1)


def shares(amount, total, most, lean, full):
    portions = [(1 << 20) // math.isqrt(rank ** lean) + 1 for rank in range(1, amount + 1)]
    largest = most if full else min(most, max(-(-total // amount), total * portions[0] // sum(portions)))
    least = 1 if total - largest >= amount - 1 else 0
    holding, rest = [largest] + [least] * (amount - 1), total - largest - least * (amount - 1)
    while rest > 0:
        free = [i for i in range(1, amount) if holding[i] < largest] or [i for i in range(1, amount) if holding[i] < most]
        mass, budget = sum([portions[i] for i in free]), rest
        for i in free:
            addition = min(most - holding[i], max(1, budget * portions[i] // mass), rest)
            holding[i] = holding[i] + addition
            rest = rest - addition
    return np.array(holding)


def bell_draw(rng, shape, scale, bound, split=(), kind=jnp.bfloat16):
    drawn = jax.random.normal(rng, shape, jnp.float32) * scale
    if len(split) > 0:
        drawn = shard_levels(rng, shape, split, -0.22, 0.18) * drawn
    return jnp.clip(drawn, min=-bound, max=bound).astype(kind)


def setup_inputs(seed: int = 0, part: int = 0) -> dict:
    splits = jax.random.split(jax.random.key(seed), 8)
    own_keys = jax.random.split(jax.random.fold_in(splits[7], part), 8)
    velocity = bell_draw(own_keys[0], (TPTS, 3, NX, NY, NZ), 0.5, 4.0, ((0, 2), (2, 4), (3, 2)), jnp.float32)
    moved_image = bell_draw(own_keys[1], (TPTS, NX, NY, NZ), 1.0, 6.0, ((0, 2), (1, 4), (2, 2)), jnp.float32)
    residual_weight = bell_draw(own_keys[2], (TPTS, NX, NY, NZ), 1.0, 6.0, ((0, 2), (1, 4), (2, 2)), jnp.float32)
    mark_values = bell_draw(own_keys[3], (LMROWS, 3, NZ), 1.0, 6.0, ((0, 16),))
    mark_brick_keys = jax.random.split(jax.random.fold_in(own_keys[4], 1), LMROWS // (LM_DEV * TPTS // N_TA))
    mark_brick_turns = jax.random.permutation(jax.random.fold_in(own_keys[4], 3), LMROWS // (LM_DEV * TPTS // N_TA))
    mark_brick = jax.vmap(lambda own, number: shared_out(jax.random.fold_in(own_keys[4], 2), own, number, LM_DEV * TPTS // N_TA, N_GX, 1, CAP, 2))(mark_brick_keys, mark_brick_turns).reshape((LMROWS, 1))
    mark_cell = place_ends(jax.random.randint(own_keys[5], (LMROWS, 1), 0, CX * CY), jax.random.fold_in(own_keys[5], 1), 0, (CX * CY) - 1).astype(jnp.int32)
    band_widths = jax.random.randint(splits[6], (3,), 3, BMAX + 1).astype(jnp.int32)
    return {"velocity": velocity, "moved_image": moved_image, "residual_weight": residual_weight, "mark_values": mark_values, "mark_brick": mark_brick, "mark_cell": mark_cell, "band_widths": band_widths}


def tent_weights(offsets, width):
    spread = jnp.abs(offsets).astype(jnp.float32)
    widthf = width.astype(jnp.float32)
    inside = jnp.where(jnp.abs(offsets) <= width, (widthf + 1.0 - spread) / ((widthf + 1.0) * (widthf + 1.0)), 0.0)
    return inside + jnp.where(offsets == 0, 0.5, 0.0).astype(jnp.float32)


def square_matrix(count, width):
    indices = jnp.arange(count, dtype=jnp.int32)
    return tent_weights(indices[:, None] - indices[None, :], width)


def reference(velocity, moved_image, residual_weight, mark_values, mark_brick, mark_cell, band_widths):
    padded = jnp.pad(moved_image, ((0, 0), (1, 1), (1, 1), (1, 1)))
    slope_x = (padded[:, 2:, 1:-1, 1:-1] - padded[:, :-2, 1:-1, 1:-1]) * 0.5
    slope_y = (padded[:, 1:-1, 2:, 1:-1] - padded[:, 1:-1, :-2, 1:-1]) * 0.5
    slope_z = (padded[:, 1:-1, 1:-1, 2:] - padded[:, 1:-1, 1:-1, :-2]) * 0.5
    force = residual_weight[:, None] * jnp.stack([slope_x, slope_y, slope_z], axis=1)
    per_device = LM_DEV * TPTS // N_TA
    rowids = jnp.arange(LMROWS, dtype=jnp.int32)
    source_y = (rowids // (N_TA * per_device)) % N_GY
    source_t = (rowids // per_device) % N_TA
    timepoint = source_t * (TPTS // N_TA) + (rowids % per_device) // LM_DEV
    line_x = mark_brick[:, 0] * CX + mark_cell[:, 0] // CY
    line_y = source_y * CY + mark_cell[:, 0] % CY
    linear = ((timepoint * NX + line_x) * NY + line_y).astype(jnp.int32)
    landed = jax.ops.segment_sum(mark_values.reshape(LMROWS, 3 * NZ).astype(jnp.float32), linear, num_segments=TPTS * NX * NY)
    landed = landed.reshape(TPTS, NX, NY, 3, NZ).transpose(0, 3, 1, 2, 4)
    total = force + landed
    high = lax.Precision.HIGHEST
    smoothed = jnp.einsum('ij,tcjyz->tciyz', square_matrix(NX, band_widths[0]), total, precision=high)
    smoothed = jnp.einsum('ij,tcxjz->tcxiz', square_matrix(NY, band_widths[1]), smoothed, precision=high)
    smoothed = jnp.einsum('tcxyj,ij->tcxyi', smoothed, square_matrix(NZ, band_widths[2]), precision=high)
    return velocity - smoothed
```

```python
import functools
import math

import jax
import jax.numpy as jnp
from jax import lax
from jax.experimental import pallas as pl
from jax.experimental.pallas import tpu as pltpu
from jax.sharding import PartitionSpec as P

LEVELS = 32000.0
MESH = pl.DeviceIdType.MESH


def each(start, stop, body):
    if stop - start <= 4:
        for i in range(start, stop):
            body(i)
    else:
        lax.fori_loop(start, stop, lambda i, c: (body(i), c)[1], 0)


def halves(x):
    hi = x.astype(jnp.bfloat16)
    return hi, (x - hi.astype(jnp.float32)).astype(jnp.bfloat16)


def tent(offsets, width):
    w1 = (width + 1).astype(jnp.float32)
    far = jnp.abs(offsets)
    inside = jnp.where(far <= width, (w1 - far.astype(jnp.float32)) / (w1 * w1), 0.0)
    return inside + jnp.where(offsets == 0, 0.5, 0.0)


def kernel(
    n_gx, n_gy, dims, width_ref, image_ref, weight_ref, mark_ref, brick_ref, cell_ref, out_ref,
    tx, scale_out, own, rx, scale_in, ytx, yown, yrx, edge_x, edge_y_out, edge_y, kmat, tmat,
    tx_send, rx_recv, s_send, s_recv, y_send, y_recv, ex_send, ex_recv, ey_send, ey_recv,
):
    steps, cx, cy, nz, rows = dims
    cells = cx * cy
    per = rows // steps
    lines = 2 * cells + per
    gx, gy = lax.axis_index("gx"), lax.axis_index("gy")
    left, right = gx > 0, gx < n_gx - 1
    low, high = gy > 0, gy < n_gy - 1
    barrier = pltpu.get_barrier_semaphore()

    def greet(s):
        pl.semaphore_signal(
            barrier, inc=1, device_id={"gx": lax.rem(gx + s, n_gx)}, device_id_type=MESH
        )

    each(1, n_gx, greet)

    @pl.when(low)
    def _():
        pl.semaphore_signal(barrier, inc=1, device_id={"gy": gy - 1}, device_id_type=MESH)

    @pl.when(high)
    def _():
        pl.semaphore_signal(barrier, inc=1, device_id={"gy": gy + 1}, device_id_type=MESH)

    for t in range(steps):
        for x in range(cx):
            r = t * cx + x
            edge_y_out[0, r : r + 1, :] = image_ref[t, x, 0:1, :]
            edge_y_out[1, r : r + 1, :] = image_ref[t, x, cy - 1 : cy, :]

    group = math.gcd(n_gx, 4)
    block = group * cells
    lane = lax.broadcasted_iota(jnp.int32, (1, lines), 1)
    fcell = lane & (cells - 1)
    for t in range(steps):
        is_mark = (lane >= t * per) & (lane < (t + 1) * per)
        sx = jnp.where(is_mark, brick_ref[...] * cx + cell_ref[...] // cy, gx * cx + fcell // cy)
        sy = jnp.where(is_mark, cell_ref[...] & (cy - 1), fcell & (cy - 1))

        def build(g, t=t, sx=sx, sy=sy):
            r = lax.broadcasted_iota(jnp.int32, (block, lines), 0)
            brick = gx + g * group + r // cells
            brick = jnp.where(brick >= n_gx, brick - n_gx, brick)
            x = brick * cx + (r // cy & (cx - 1))
            k = jnp.where((r & (cy - 1)) == sy, tent(x - sx, width_ref[0]), 0.0)
            hi, lo = halves(k)
            at = pl.ds(pl.multiple_of(g * block, block), block)
            kmat[t, at, 0:lines] = hi
            kmat[t, at, lines : 2 * lines] = lo

        each(0, n_gx // group, build)

    pl.semaphore_wait(barrier, n_gx - 1 + low.astype(jnp.int32) + high.astype(jnp.int32))

    def x_edge(d, plane, to):
        return pltpu.make_async_remote_copy(
            image_ref.at[:, plane], edge_x.at[d], ex_send.at[d], ex_recv.at[d],
            device_id={"gx": to}, device_id_type=MESH,
        )

    def y_edge(d, side, to):
        return pltpu.make_async_remote_copy(
            edge_y_out.at[side], edge_y.at[d], ey_send.at[d], ey_recv.at[d],
            device_id={"gy": to}, device_id_type=MESH,
        )

    exchanges = (
        (right, left, x_edge(0, cx - 1, gx + 1), edge_x, 0),
        (left, right, x_edge(1, 0, gx - 1), edge_x, 1),
        (high, low, y_edge(0, 1, gy + 1), edge_y, 0),
        (low, high, y_edge(1, 0, gy - 1), edge_y, 1),
    )
    for sends, receives, copy, buffer, d in exchanges:
        pl.when(sends)(copy.start)

        @pl.when(jnp.logical_not(receives))
        def _(buffer=buffer, d=d):
            buffer[d] = jnp.zeros(buffer.shape[1:], buffer.dtype)

    def brick_copy(k, s):
        return pltpu.make_async_remote_copy(
            tx.at[k, s], rx.at[k, s], tx_send.at[k, s], rx_recv.at[k, s],
            device_id={"gx": lax.rem(gx + s, n_gx)}, device_id_type=MESH,
        )

    def scale_copy(k, s):
        return pltpu.make_async_remote_copy(
            scale_out.at[k, s], scale_in.at[k, s], s_send.at[k, s], s_recv.at[k, s],
            device_id={"gx": lax.rem(gx + s, n_gx)}, device_id_type=MESH,
        )

    def send(k, s):
        brick_copy(k, s).start()
        scale_copy(k, s).start()

    def receive(k, s):
        brick_copy(k, s).wait_recv()
        scale_copy(k, s).wait_recv()
        return rx[k, s].astype(jnp.int32).astype(jnp.float32) * scale_in[k, s]

    def settle(k, s):
        brick_copy(k, s).wait_send()
        scale_copy(k, s).wait_send()

    order = [(t, c) for c in (2, 0, 1) for t in range(steps)]
    for k, (t, c) in enumerate(order):
        if k == steps:
            for _, receives, copy, _, _ in exchanges:
                pl.when(receives)(copy.wait_recv)
        m = image_ref[t]
        if c == 2:
            flat = m.reshape(cells, nz)
            z = lax.broadcasted_iota(jnp.int32, (cells, nz), 1)
            after = jnp.where(z == nz - 1, 0.0, pltpu.roll(flat, nz - 1, 1))
            before = jnp.where(z == 0, 0.0, pltpu.roll(flat, 1, 1))
            slope = after - before
        elif c == 0:
            after = jnp.concatenate([m[1:], edge_x[1, t][None]], axis=0)
            before = jnp.concatenate([edge_x[0, t][None], m[:-1]], axis=0)
            slope = (after - before).reshape(cells, nz)
        else:
            flat = m.reshape(cells, nz)
            y = lax.broadcasted_iota(jnp.int32, (cy, nz), 0)
            parts = []
            for x in range(cx):
                r = t * cx + x
                after = jnp.where(y == cy - 1, edge_y[1, r : r + 1, :], pltpu.roll(m[x], cy - 1, 0))
                before = jnp.where(y == 0, edge_y[0, r : r + 1, :], pltpu.roll(m[x], 1, 0))
                parts.append(after - before)
            slope = jnp.concatenate(parts, axis=0)
        hi, lo = halves(weight_ref[t].reshape(cells, nz) * slope * 0.5)
        marks = mark_ref[c, t * per : (t + 1) * per, :]
        pieces = [hi, lo]
        pieces.insert(0 if t == 0 else 2, marks)
        b = jnp.concatenate(pieces, axis=0)
        b = jnp.concatenate([b, b], axis=0)

        def spread(g, k=k, t=t, b=b):
            at = pl.ds(pl.multiple_of(g * block, block), block)
            p = jnp.dot(kmat[t, at, :], b, preferred_element_type=jnp.float32)
            for i in range(group):
                piece = p[i * cells : (i + 1) * cells]
                s = g * group + i
                top = jnp.maximum(jnp.max(jnp.abs(piece), axis=0, keepdims=True), 1e-30)
                tx[k, s] = jnp.round(piece * (LEVELS / top)).astype(jnp.int32).astype(jnp.int16)
                scale_out[k, s] = top * (1.0 / LEVELS)
                if i == 0:
                    if n_gx == group:
                        own[k] = piece
                    else:

                        @pl.when(g == 0)
                        def _():
                            own[k] = piece

        each(0, n_gx // group, spread)
        each(1, n_gx, lambda s, k=k: send(k, s))

    zi = lax.broadcasted_iota(jnp.int32, (nz, nz), 0)
    zj = lax.broadcasted_iota(jnp.int32, (nz, nz), 1)
    tmat[...] = (
        jnp.maximum(width_ref[2] + 1 - jnp.abs(zi - zj), 0).astype(jnp.float32).astype(jnp.bfloat16)
    )
    wz = jnp.full((1, nz), (width_ref[2] + 1).astype(jnp.float32), jnp.float32)
    inv = 1.0 / (wz * wz)

    r = lax.broadcasted_iota(jnp.int32, (3 * cells, cells), 0)
    q = lax.broadcasted_iota(jnp.int32, (3 * cells, cells), 1)
    which = r // cells
    shift = jnp.where(which == 1, cy, jnp.where(which == 2, -cy, 0))
    same = (r // cy & (cx - 1)) == q // cy
    ymat = jnp.where(same, tent((r & (cy - 1)) + shift - (q & (cy - 1)), width_ref[1]), 0.0)
    yhi, ylo = halves(ymat)
    ymats = jnp.concatenate([yhi, yhi, ylo], axis=1)

    def y_copy(k, d, to):
        return pltpu.make_async_remote_copy(
            ytx.at[k, d], yrx.at[k, d], y_send.at[k, d], y_recv.at[k, d],
            device_id={"gy": to}, device_id_type=MESH,
        )

    def finish(k):
        t, c = order[k]
        out_ref[t, c] = yown[k].reshape(cx, cy, nz)
        for d, receives in ((0, low), (1, high)):

            @pl.when(receives)
            def _(d=d):
                y_copy(k, d, gy).wait_recv()
                out_ref[t, c] += yrx[k, d].astype(jnp.float32).reshape(cx, cy, nz)

    for k in range(len(order)):
        acc = own[k]
        if n_gx <= 4:
            for s in range(1, n_gx):
                acc = acc + receive(k, s)
        else:

            acc = lax.fori_loop(1, n_gx, lambda s, acc, k=k: acc + receive(k, s), acc)
        hi, lo = halves(acc)
        wide = jnp.dot(
            jnp.concatenate([hi, lo], axis=0), tmat[...], preferred_element_type=jnp.float32
        )
        zs = 0.5 * acc + (wide[:cells] + wide[cells:]) * inv
        hi, lo = halves(zs)
        v = jnp.dot(
            ymats, jnp.concatenate([hi, lo, hi], axis=0), preferred_element_type=jnp.float32
        )
        yown[k] = v[:cells]
        ytx[k, 0] = v[cells : 2 * cells].astype(jnp.bfloat16)
        ytx[k, 1] = v[2 * cells :].astype(jnp.bfloat16)
        pl.when(high)(y_copy(k, 0, gy + 1).start)
        pl.when(low)(y_copy(k, 1, gy - 1).start)
        if k > 0:
            finish(k - 1)
    finish(len(order) - 1)

    for sends, _, copy, _, _ in exchanges:
        pl.when(sends)(copy.wait_send)
    for k in range(len(order)):
        each(1, n_gx, lambda s, k=k: settle(k, s))
        pl.when(high)(y_copy(k, 0, gy).wait_send)
        pl.when(low)(y_copy(k, 1, gy).wait_send)


def shards(velocity, moved_image, residual_weight, mark_values, mark_brick, mark_cell, band_widths):
    n_gx, n_gy = lax.axis_size("gx"), lax.axis_size("gy")
    steps, cx, cy, nz = moved_image.shape
    rows = mark_values.shape[0]
    cells = cx * cy
    chunks = 3 * steps
    lines = 2 * cells + rows // steps
    f32, bf16 = jnp.float32, jnp.bfloat16
    dma = pltpu.SemaphoreType.DMA
    vmem = pl.BlockSpec(memory_space=pltpu.VMEM)
    smoothed = pl.pallas_call(
        functools.partial(kernel, n_gx, n_gy, (steps, cx, cy, nz, rows)),
        out_shape=jax.ShapeDtypeStruct(velocity.shape, f32),
        in_specs=[pl.BlockSpec(memory_space=pltpu.SMEM)] + [vmem] * 5,
        out_specs=vmem,
        scratch_shapes=[
            pltpu.VMEM((chunks, n_gx, cells, nz), jnp.int16),
            pltpu.VMEM((chunks, n_gx, 1, nz), f32),
            pltpu.VMEM((chunks, cells, nz), f32),
            pltpu.VMEM((chunks, n_gx, cells, nz), jnp.int16),
            pltpu.VMEM((chunks, n_gx, 1, nz), f32),
            pltpu.VMEM((chunks, 2, cells, nz), bf16),
            pltpu.VMEM((chunks, cells, nz), f32),
            pltpu.VMEM((chunks, 2, cells, nz), bf16),
            pltpu.VMEM((2, steps, cy, nz), f32),
            pltpu.VMEM((2, steps * cx, nz), f32),
            pltpu.VMEM((2, steps * cx, nz), f32),
            pltpu.VMEM((steps, n_gx * cells, 2 * lines), bf16),
            pltpu.VMEM((nz, nz), bf16),
            dma((chunks, n_gx)),
            dma((chunks, n_gx)),
            dma((chunks, n_gx)),
            dma((chunks, n_gx)),
            dma((chunks, 2)),
            dma((chunks, 2)),
            dma((2,)),
            dma((2,)),
            dma((2,)),
            dma((2,)),
        ],
        compiler_params=pltpu.CompilerParams(
            collective_id=0, has_side_effects=True, vmem_limit_bytes=40 * 2**20
        ),
        cost_estimate=pl.CostEstimate(
            flops=4 * 10**8, bytes_accessed=2 * 10**6, transcendentals=0
        ),
    )(
        band_widths,
        moved_image,
        residual_weight,
        mark_values.transpose(1, 0, 2),
        mark_brick.reshape(1, rows),
        mark_cell.reshape(1, rows),
    )
    return velocity - smoothed


def solution(mesh):
    return jax.shard_map(
        shards,
        mesh=mesh,
        in_specs=(
            P(("group", "ta"), None, "gx", "gy", None),
            P(("group", "ta"), "gx", "gy", None),
            P(("group", "ta"), "gx", "gy", None),
            P(("group", "gx", "gy", "ta"), None, None),
            P(("group", "gx", "gy", "ta"), None),
            P(("group", "gx", "gy", "ta"), None),
            P(),
        ),
        out_specs=P(("group", "ta"), None, "gx", "gy", None),
        check_vma=False,
    )
```

```python
import functools
import math

import jax
import jax.numpy as jnp
from jax import lax
from jax.experimental import pallas as pl
from jax.experimental.pallas import tpu as pltpu
from jax.sharding import PartitionSpec as P

LEVELS = 32000.0
MESH = pl.DeviceIdType.MESH


def each(start, stop, body):
    if stop - start <= 4:
        for i in range(start, stop):
            body(i)
    else:
        lax.fori_loop(start, stop, lambda i, c: (body(i), c)[1], 0)


def halves(x):
    hi = x.astype(jnp.bfloat16)
    return hi, (x - hi.astype(jnp.float32)).astype(jnp.bfloat16)


def tent(offsets, width):
    w1 = (width + 1).astype(jnp.float32)
    far = jnp.abs(offsets)
    inside = jnp.where(far <= width, (w1 - far.astype(jnp.float32)) / (w1 * w1), 0.0)
    return inside + jnp.where(offsets == 0, 0.5, 0.0)


def kernel(
    n_gx, n_gy, dims, width_hbm, image_hbm, weight_hbm, mark_hbm, brick_hbm, cell_hbm, out_hbm,
    width_ref, image_ref, weight_ref, mark_ref, brick_ref, cell_ref, out_ref, load_sem, store_sem,
    tx, scale_out, own, rx, scale_in, ytx, yown, yrx, edge_x, edge_y_out, edge_y, kmat, tmat,
    tx_send, rx_recv, s_send, s_recv, y_send, y_recv, ex_send, ex_recv, ey_send, ey_recv,
):
    steps, cx, cy, nz, rows = dims
    cells = cx * cy
    per = rows // steps
    lines = 2 * cells + per
    gx, gy = lax.axis_index("gx"), lax.axis_index("gy")
    left, right = gx > 0, gx < n_gx - 1
    low, high = gy > 0, gy < n_gy - 1
    barrier = pltpu.get_barrier_semaphore()

    names = ("width", "brick", "cell", "image", "weight", "mark0", "mark1", "mark2")
    pairs = [(width_hbm, width_ref), (brick_hbm, brick_ref), (cell_hbm, cell_ref)]
    pairs += [(image_hbm, image_ref), (weight_hbm, weight_ref)]
    pairs += [(mark_hbm.at[c], mark_ref.at[c]) for c in range(3)]
    loads = {
        name: pltpu.make_async_copy(src, dst, load_sem.at[i])
        for i, (name, (src, dst)) in enumerate(zip(names, pairs))
    }
    for name in ("image", "width", "brick", "cell", "weight", "mark2", "mark0", "mark1"):
        loads[name].start()

    def greet(s):
        pl.semaphore_signal(
            barrier, inc=1, device_id={"gx": lax.rem(gx + s, n_gx)}, device_id_type=MESH
        )

    each(1, n_gx, greet)

    @pl.when(low)
    def _():
        pl.semaphore_signal(barrier, inc=1, device_id={"gy": gy - 1}, device_id_type=MESH)

    @pl.when(high)
    def _():
        pl.semaphore_signal(barrier, inc=1, device_id={"gy": gy + 1}, device_id_type=MESH)

    loads["image"].wait()
    for t in range(steps):
        for x in range(cx):
            r = t * cx + x
            edge_y_out[0, r : r + 1, :] = image_ref[t, x, 0:1, :]
            edge_y_out[1, r : r + 1, :] = image_ref[t, x, cy - 1 : cy, :]

    pl.semaphore_wait(barrier, n_gx - 1 + low.astype(jnp.int32) + high.astype(jnp.int32))

    def x_edge(d, plane, to):
        return pltpu.make_async_remote_copy(
            image_ref.at[:, plane], edge_x.at[d], ex_send.at[d], ex_recv.at[d],
            device_id={"gx": to}, device_id_type=MESH,
        )

    def y_edge(d, side, to):
        return pltpu.make_async_remote_copy(
            edge_y_out.at[side], edge_y.at[d], ey_send.at[d], ey_recv.at[d],
            device_id={"gy": to}, device_id_type=MESH,
        )

    exchanges = (
        (right, left, x_edge(0, cx - 1, gx + 1), edge_x, 0),
        (left, right, x_edge(1, 0, gx - 1), edge_x, 1),
        (high, low, y_edge(0, 1, gy + 1), edge_y, 0),
        (low, high, y_edge(1, 0, gy - 1), edge_y, 1),
    )
    for sends, receives, copy, buffer, d in exchanges:
        pl.when(sends)(copy.start)

        @pl.when(jnp.logical_not(receives))
        def _(buffer=buffer, d=d):
            buffer[d] = jnp.zeros(buffer.shape[1:], buffer.dtype)

    for name in ("width", "brick", "cell"):
        loads[name].wait()
    group = math.gcd(n_gx, 4)
    block = group * cells
    lane = lax.broadcasted_iota(jnp.int32, (1, lines), 1)
    fcell = lane & (cells - 1)
    for t in range(steps):
        is_mark = (lane >= t * per) & (lane < (t + 1) * per)
        sx = jnp.where(is_mark, brick_ref[...] * cx + cell_ref[...] // cy, gx * cx + fcell // cy)
        sy = jnp.where(is_mark, cell_ref[...] & (cy - 1), fcell & (cy - 1))

        def build(g, t=t, sx=sx, sy=sy):
            r = lax.broadcasted_iota(jnp.int32, (block, lines), 0)
            brick = gx + g * group + r // cells
            brick = jnp.where(brick >= n_gx, brick - n_gx, brick)
            x = brick * cx + (r // cy & (cx - 1))
            k = jnp.where((r & (cy - 1)) == sy, tent(x - sx, width_ref[0]), 0.0)
            hi, lo = halves(k)
            at = pl.ds(pl.multiple_of(g * block, block), block)
            kmat[t, at, 0:lines] = hi
            kmat[t, at, lines : 2 * lines] = lo

        each(0, n_gx // group, build)

    def brick_copy(k, s):
        return pltpu.make_async_remote_copy(
            tx.at[k, s], rx.at[k, s], tx_send.at[k, s], rx_recv.at[k, s],
            device_id={"gx": lax.rem(gx + s, n_gx)}, device_id_type=MESH,
        )

    def scale_copy(k, s):
        return pltpu.make_async_remote_copy(
            scale_out.at[k, s], scale_in.at[k, s], s_send.at[k, s], s_recv.at[k, s],
            device_id={"gx": lax.rem(gx + s, n_gx)}, device_id_type=MESH,
        )

    def send(k, s):
        brick_copy(k, s).start()
        scale_copy(k, s).start()

    def receive(k, s):
        brick_copy(k, s).wait_recv()
        scale_copy(k, s).wait_recv()
        return rx[k, s].astype(jnp.int32).astype(jnp.float32) * scale_in[k, s]

    def settle(k, s):
        brick_copy(k, s).wait_send()
        scale_copy(k, s).wait_send()

    order = [(t, c) for c in (2, 0, 1) for t in range(steps)]
    for k, (t, c) in enumerate(order):
        if k == steps:
            for _, receives, copy, _, _ in exchanges:
                pl.when(receives)(copy.wait_recv)
        if k == 0:
            loads["weight"].wait()
        if t == 0:
            loads[names[5 + c]].wait()
        m = image_ref[t]
        if c == 2:
            flat = m.reshape(cells, nz)
            z = lax.broadcasted_iota(jnp.int32, (cells, nz), 1)
            after = jnp.where(z == nz - 1, 0.0, pltpu.roll(flat, nz - 1, 1))
            before = jnp.where(z == 0, 0.0, pltpu.roll(flat, 1, 1))
            slope = after - before
        elif c == 0:
            after = jnp.concatenate([m[1:], edge_x[1, t][None]], axis=0)
            before = jnp.concatenate([edge_x[0, t][None], m[:-1]], axis=0)
            slope = (after - before).reshape(cells, nz)
        else:
            flat = m.reshape(cells, nz)
            y = lax.broadcasted_iota(jnp.int32, (cy, nz), 0)
            parts = []
            for x in range(cx):
                r = t * cx + x
                after = jnp.where(y == cy - 1, edge_y[1, r : r + 1, :], pltpu.roll(m[x], cy - 1, 0))
                before = jnp.where(y == 0, edge_y[0, r : r + 1, :], pltpu.roll(m[x], 1, 0))
                parts.append(after - before)
            slope = jnp.concatenate(parts, axis=0)
        hi, lo = halves(weight_ref[t].reshape(cells, nz) * slope * 0.5)
        marks = mark_ref[c, t * per : (t + 1) * per, :]
        pieces = [hi, lo]
        pieces.insert(0 if t == 0 else 2, marks)
        b = jnp.concatenate(pieces, axis=0)
        b = jnp.concatenate([b, b], axis=0)

        def spread(g, k=k, t=t, b=b):
            at = pl.ds(pl.multiple_of(g * block, block), block)
            p = jnp.dot(kmat[t, at, :], b, preferred_element_type=jnp.float32)
            for i in range(group):
                piece = p[i * cells : (i + 1) * cells]
                s = g * group + i
                top = jnp.maximum(jnp.max(jnp.abs(piece), axis=0, keepdims=True), 1e-30)
                tx[k, s] = jnp.round(piece * (LEVELS / top)).astype(jnp.int32).astype(jnp.int16)
                scale_out[k, s] = top * (1.0 / LEVELS)
                if i == 0:
                    if n_gx == group:
                        own[k] = piece
                    else:

                        @pl.when(g == 0)
                        def _():
                            own[k] = piece

        each(0, n_gx // group, spread)
        each(1, n_gx, lambda s, k=k: send(k, s))

    zi = lax.broadcasted_iota(jnp.int32, (nz, nz), 0)
    zj = lax.broadcasted_iota(jnp.int32, (nz, nz), 1)
    tmat[...] = (
        jnp.maximum(width_ref[2] + 1 - jnp.abs(zi - zj), 0).astype(jnp.float32).astype(jnp.bfloat16)
    )
    wz = jnp.full((1, nz), (width_ref[2] + 1).astype(jnp.float32), jnp.float32)
    inv = 1.0 / (wz * wz)

    r = lax.broadcasted_iota(jnp.int32, (3 * cells, cells), 0)
    q = lax.broadcasted_iota(jnp.int32, (3 * cells, cells), 1)
    which = r // cells
    shift = jnp.where(which == 1, cy, jnp.where(which == 2, -cy, 0))
    same = (r // cy & (cx - 1)) == q // cy
    ymat = jnp.where(same, tent((r & (cy - 1)) + shift - (q & (cy - 1)), width_ref[1]), 0.0)
    yhi, ylo = halves(ymat)
    ymats = jnp.concatenate([yhi, yhi, ylo], axis=1)

    def y_copy(k, d, to):
        return pltpu.make_async_remote_copy(
            ytx.at[k, d], yrx.at[k, d], y_send.at[k, d], y_recv.at[k, d],
            device_id={"gy": to}, device_id_type=MESH,
        )

    def store(k):
        t, c = order[k]
        return pltpu.make_async_copy(out_ref.at[t, c], out_hbm.at[t, c], store_sem.at[k])

    def finish(k):
        t, c = order[k]
        out_ref[t, c] = yown[k].reshape(cx, cy, nz)
        for d, receives in ((0, low), (1, high)):

            @pl.when(receives)
            def _(d=d):
                y_copy(k, d, gy).wait_recv()
                out_ref[t, c] += yrx[k, d].astype(jnp.float32).reshape(cx, cy, nz)

        store(k).start()

    for k in range(len(order)):
        acc = own[k]
        if n_gx <= 4:
            for s in range(1, n_gx):
                acc = acc + receive(k, s)
        else:

            acc = lax.fori_loop(1, n_gx, lambda s, acc, k=k: acc + receive(k, s), acc)
        hi, lo = halves(acc)
        wide = jnp.dot(
            jnp.concatenate([hi, lo], axis=0), tmat[...], preferred_element_type=jnp.float32
        )
        zs = 0.5 * acc + (wide[:cells] + wide[cells:]) * inv
        hi, lo = halves(zs)
        v = jnp.dot(
            ymats, jnp.concatenate([hi, lo, hi], axis=0), preferred_element_type=jnp.float32
        )
        yown[k] = v[:cells]
        ytx[k, 0] = v[cells : 2 * cells].astype(jnp.bfloat16)
        ytx[k, 1] = v[2 * cells :].astype(jnp.bfloat16)
        pl.when(high)(y_copy(k, 0, gy + 1).start)
        pl.when(low)(y_copy(k, 1, gy - 1).start)
        if k > 0:
            finish(k - 1)
    finish(len(order) - 1)

    for sends, _, copy, _, _ in exchanges:
        pl.when(sends)(copy.wait_send)
    for k in range(len(order)):
        each(1, n_gx, lambda s, k=k: settle(k, s))
        pl.when(high)(y_copy(k, 0, gy).wait_send)
        pl.when(low)(y_copy(k, 1, gy).wait_send)
        store(k).wait()


def shards(velocity, moved_image, residual_weight, mark_values, mark_brick, mark_cell, band_widths):
    n_gx, n_gy = lax.axis_size("gx"), lax.axis_size("gy")
    steps, cx, cy, nz = moved_image.shape
    rows = mark_values.shape[0]
    cells = cx * cy
    chunks = 3 * steps
    lines = 2 * cells + rows // steps
    f32, bf16 = jnp.float32, jnp.bfloat16
    dma = pltpu.SemaphoreType.DMA
    smoothed = pl.pallas_call(
        functools.partial(kernel, n_gx, n_gy, (steps, cx, cy, nz, rows)),
        out_shape=jax.ShapeDtypeStruct(velocity.shape, f32),
        in_specs=[pl.BlockSpec(memory_space=pltpu.HBM)] * 6,
        out_specs=pl.BlockSpec(memory_space=pltpu.HBM),
        scratch_shapes=[
            pltpu.SMEM(band_widths.shape, jnp.int32),
            pltpu.VMEM(moved_image.shape, f32),
            pltpu.VMEM(residual_weight.shape, f32),
            pltpu.VMEM((3, rows, nz), bf16),
            pltpu.VMEM((1, rows), jnp.int32),
            pltpu.VMEM((1, rows), jnp.int32),
            pltpu.VMEM(velocity.shape, f32),
            dma((8,)),
            dma((chunks,)),
            pltpu.VMEM((chunks, n_gx, cells, nz), jnp.int16),
            pltpu.VMEM((chunks, n_gx, 1, nz), f32),
            pltpu.VMEM((chunks, cells, nz), f32),
            pltpu.VMEM((chunks, n_gx, cells, nz), jnp.int16),
            pltpu.VMEM((chunks, n_gx, 1, nz), f32),
            pltpu.VMEM((chunks, 2, cells, nz), bf16),
            pltpu.VMEM((chunks, cells, nz), f32),
            pltpu.VMEM((chunks, 2, cells, nz), bf16),
            pltpu.VMEM((2, steps, cy, nz), f32),
            pltpu.VMEM((2, steps * cx, nz), f32),
            pltpu.VMEM((2, steps * cx, nz), f32),
            pltpu.VMEM((steps, n_gx * cells, 2 * lines), bf16),
            pltpu.VMEM((nz, nz), bf16),
            dma((chunks, n_gx)),
            dma((chunks, n_gx)),
            dma((chunks, n_gx)),
            dma((chunks, n_gx)),
            dma((chunks, 2)),
            dma((chunks, 2)),
            dma((2,)),
            dma((2,)),
            dma((2,)),
            dma((2,)),
        ],
        compiler_params=pltpu.CompilerParams(
            collective_id=0, has_side_effects=True, vmem_limit_bytes=63 * 2**20
        ),
        cost_estimate=pl.CostEstimate(
            flops=4 * 10**8, bytes_accessed=2 * 10**6, transcendentals=0
        ),
    )(
        band_widths,
        moved_image,
        residual_weight,
        mark_values.transpose(1, 0, 2),
        mark_brick.reshape(1, rows),
        mark_cell.reshape(1, rows),
    )
    return velocity - smoothed


def solution(mesh):
    return jax.shard_map(
        shards,
        mesh=mesh,
        in_specs=(
            P(("group", "ta"), None, "gx", "gy", None),
            P(("group", "ta"), "gx", "gy", None),
            P(("group", "ta"), "gx", "gy", None),
            P(("group", "gx", "gy", "ta"), None, None),
            P(("group", "gx", "gy", "ta"), None),
            P(("group", "gx", "gy", "ta"), None),
            P(),
        ),
        out_specs=P(("group", "ta"), None, "gx", "gy", None),
        check_vma=False,
    )
```

```python
import functools
import math

import jax
import jax.numpy as jnp
from jax import lax
from jax.experimental import pallas as pl
from jax.experimental.pallas import tpu as pltpu
from jax.sharding import PartitionSpec as P

LEVELS = 32000.0
LAG = 2
MESH = pl.DeviceIdType.MESH


def each(start, stop, body):
    if stop - start <= 4:
        for i in range(start, stop):
            body(i)
    else:
        lax.fori_loop(start, stop, lambda i, c: (body(i), c)[1], 0)


def halves(x):
    hi = x.astype(jnp.bfloat16)
    return hi, (x - hi.astype(jnp.float32)).astype(jnp.bfloat16)


def tent(offsets, width):
    w1 = (width + 1).astype(jnp.float32)
    far = jnp.abs(offsets)
    inside = jnp.where(far <= width, (w1 - far.astype(jnp.float32)) / (w1 * w1), 0.0)
    return inside + jnp.where(offsets == 0, 0.5, 0.0)


def kernel(
    n_gx, n_gy, dims, width_hbm, image_hbm, weight_hbm, mark_hbm, brick_hbm, cell_hbm, out_hbm,
    width_ref, image_ref, weight_ref, mark_ref, brick_ref, cell_ref, out_ref, load_sem, store_sem,
    tx, scale_out, own, rx, scale_in, ytx, yown, yrx, edge_x, edge_y_out, edge_y, kmat, tmat,
    tx_send, rx_recv, s_send, s_recv, y_send, y_recv, ex_send, ex_recv, ey_send, ey_recv,
):
    steps, cx, cy, nz, rows = dims
    cells = cx * cy
    per = rows // steps
    lines = 2 * cells + per
    gx, gy = lax.axis_index("gx"), lax.axis_index("gy")
    left, right = gx > 0, gx < n_gx - 1
    low, high = gy > 0, gy < n_gy - 1
    barrier = pltpu.get_barrier_semaphore()

    names = ("width", "brick", "cell", "image", "weight", "mark0", "mark1", "mark2")
    pairs = [(width_hbm, width_ref), (brick_hbm, brick_ref), (cell_hbm, cell_ref)]
    pairs += [(image_hbm, image_ref), (weight_hbm, weight_ref)]
    pairs += [(mark_hbm.at[c], mark_ref.at[c]) for c in range(3)]
    loads = {
        name: pltpu.make_async_copy(src, dst, load_sem.at[i])
        for i, (name, (src, dst)) in enumerate(zip(names, pairs))
    }
    for name in ("image", "width", "brick", "cell", "weight", "mark2", "mark0", "mark1"):
        loads[name].start()

    def greet(s):
        pl.semaphore_signal(
            barrier, inc=1, device_id={"gx": lax.rem(gx + s, n_gx)}, device_id_type=MESH
        )

    each(1, n_gx, greet)

    @pl.when(low)
    def _():
        pl.semaphore_signal(barrier, inc=1, device_id={"gy": gy - 1}, device_id_type=MESH)

    @pl.when(high)
    def _():
        pl.semaphore_signal(barrier, inc=1, device_id={"gy": gy + 1}, device_id_type=MESH)

    def x_edge(d, plane, to):
        return pltpu.make_async_remote_copy(
            image_ref.at[:, plane], edge_x.at[d], ex_send.at[d], ex_recv.at[d],
            device_id={"gx": to}, device_id_type=MESH,
        )

    def y_edge(d, side, to):
        return pltpu.make_async_remote_copy(
            edge_y_out.at[side], edge_y.at[d], ey_send.at[d], ey_recv.at[d],
            device_id={"gy": to}, device_id_type=MESH,
        )

    exchanges = (
        (right, left, x_edge(0, cx - 1, gx + 1), edge_x, 0),
        (left, right, x_edge(1, 0, gx - 1), edge_x, 1),
        (high, low, y_edge(0, 1, gy + 1), edge_y, 0),
        (low, high, y_edge(1, 0, gy - 1), edge_y, 1),
    )
    for name in ("width", "brick", "cell"):
        loads[name].wait()
    group = math.gcd(n_gx, 4)
    block = group * cells
    lane = lax.broadcasted_iota(jnp.int32, (1, lines), 1)
    fcell = lane & (cells - 1)
    for t in range(steps):
        is_mark = (lane >= t * per) & (lane < (t + 1) * per)
        sx = jnp.where(is_mark, brick_ref[...] * cx + cell_ref[...] // cy, gx * cx + fcell // cy)
        sy = jnp.where(is_mark, cell_ref[...] & (cy - 1), fcell & (cy - 1))

        def build(g, t=t, sx=sx, sy=sy):
            r = lax.broadcasted_iota(jnp.int32, (block, lines), 0)
            brick = gx + g * group + r // cells
            brick = jnp.where(brick >= n_gx, brick - n_gx, brick)
            x = brick * cx + (r // cy & (cx - 1))
            k = jnp.where((r & (cy - 1)) == sy, tent(x - sx, width_ref[0]), 0.0)
            hi, lo = halves(k)
            at = pl.ds(pl.multiple_of(g * block, block), block)
            kmat[t, at, 0:lines] = hi
            kmat[t, at, lines : 2 * lines] = lo

        each(0, n_gx // group, build)

    loads["image"].wait()
    for t in range(steps):
        for x in range(cx):
            r = t * cx + x
            edge_y_out[0, r : r + 1, :] = image_ref[t, x, 0:1, :]
            edge_y_out[1, r : r + 1, :] = image_ref[t, x, cy - 1 : cy, :]

    def brick_copy(k, s):
        return pltpu.make_async_remote_copy(
            tx.at[k, s], rx.at[k, s], tx_send.at[k, s], rx_recv.at[k, s],
            device_id={"gx": lax.rem(gx + s, n_gx)}, device_id_type=MESH,
        )

    def scale_copy(k, s):
        return pltpu.make_async_remote_copy(
            scale_out.at[k, s], scale_in.at[k, s], s_send.at[k, s], s_recv.at[k, s],
            device_id={"gx": lax.rem(gx + s, n_gx)}, device_id_type=MESH,
        )

    def send(k, s):
        brick_copy(k, s).start()
        scale_copy(k, s).start()

    def receive(k, s):
        brick_copy(k, s).wait_recv()
        scale_copy(k, s).wait_recv()
        return rx[k, s].astype(jnp.int32).astype(jnp.float32) * scale_in[k, s]

    def settle(k, s):
        brick_copy(k, s).wait_send()
        scale_copy(k, s).wait_send()

    def meet():
        pl.semaphore_wait(barrier, n_gx - 1 + low.astype(jnp.int32) + high.astype(jnp.int32))

        for sends, receives, copy, buffer, d in exchanges:
            pl.when(sends)(copy.start)

            @pl.when(jnp.logical_not(receives))
            def _(buffer=buffer, d=d):
                buffer[d] = jnp.zeros(buffer.shape[1:], buffer.dtype)

    order = [(t, c) for c in (2, 0, 1) for t in range(steps)]
    for k, (t, c) in enumerate(order):
        if k == steps:
            for _, receives, copy, _, _ in exchanges:
                pl.when(receives)(copy.wait_recv)
        if k == 0:
            loads["weight"].wait()
        if t == 0:
            loads[names[5 + c]].wait()
        m = image_ref[t]
        if c == 2:
            flat = m.reshape(cells, nz)
            z = lax.broadcasted_iota(jnp.int32, (cells, nz), 1)
            after = jnp.where(z == nz - 1, 0.0, pltpu.roll(flat, nz - 1, 1))
            before = jnp.where(z == 0, 0.0, pltpu.roll(flat, 1, 1))
            slope = after - before
        elif c == 0:
            after = jnp.concatenate([m[1:], edge_x[1, t][None]], axis=0)
            before = jnp.concatenate([edge_x[0, t][None], m[:-1]], axis=0)
            slope = (after - before).reshape(cells, nz)
        else:
            flat = m.reshape(cells, nz)
            y = lax.broadcasted_iota(jnp.int32, (cy, nz), 0)
            parts = []
            for x in range(cx):
                r = t * cx + x
                after = jnp.where(y == cy - 1, edge_y[1, r : r + 1, :], pltpu.roll(m[x], cy - 1, 0))
                before = jnp.where(y == 0, edge_y[0, r : r + 1, :], pltpu.roll(m[x], 1, 0))
                parts.append(after - before)
            slope = jnp.concatenate(parts, axis=0)
        hi, lo = halves(weight_ref[t].reshape(cells, nz) * slope * 0.5)
        marks = mark_ref[c, t * per : (t + 1) * per, :]
        pieces = [hi, lo]
        pieces.insert(0 if t == 0 else 2, marks)
        b = jnp.concatenate(pieces, axis=0)
        b = jnp.concatenate([b, b], axis=0)

        def spread(g, k=k, t=t, b=b):
            at = pl.ds(pl.multiple_of(g * block, block), block)
            p = jnp.dot(kmat[t, at, :], b, preferred_element_type=jnp.float32)
            for i in range(group):
                piece = p[i * cells : (i + 1) * cells]
                s = g * group + i
                top = jnp.maximum(jnp.max(jnp.abs(piece), axis=0, keepdims=True), 1e-30)
                tx[k, s] = jnp.round(piece * (LEVELS / top)).astype(jnp.int32).astype(jnp.int16)
                scale_out[k, s] = top * (1.0 / LEVELS)
                if i == 0:
                    if n_gx == group:
                        own[k] = piece
                    else:

                        @pl.when(g == 0)
                        def _():
                            own[k] = piece

        each(0, n_gx // group, spread)
        if k == steps - 1:
            meet()
        for ready in range(steps) if k == steps - 1 else [k] if k >= steps else []:
            each(1, n_gx, lambda s, k=ready: send(k, s))

    zi = lax.broadcasted_iota(jnp.int32, (nz, nz), 0)
    zj = lax.broadcasted_iota(jnp.int32, (nz, nz), 1)
    tmat[...] = (
        jnp.maximum(width_ref[2] + 1 - jnp.abs(zi - zj), 0).astype(jnp.float32).astype(jnp.bfloat16)
    )
    wz = jnp.full((1, nz), (width_ref[2] + 1).astype(jnp.float32), jnp.float32)
    inv = 1.0 / (wz * wz)

    r = lax.broadcasted_iota(jnp.int32, (3 * cells, cells), 0)
    q = lax.broadcasted_iota(jnp.int32, (3 * cells, cells), 1)
    which = r // cells
    shift = jnp.where(which == 1, cy, jnp.where(which == 2, -cy, 0))
    same = (r // cy & (cx - 1)) == q // cy
    ymat = jnp.where(same, tent((r & (cy - 1)) + shift - (q & (cy - 1)), width_ref[1]), 0.0)
    yhi, ylo = halves(ymat)
    ymats = jnp.concatenate([yhi, yhi, ylo], axis=1)

    def y_copy(k, d, to):
        return pltpu.make_async_remote_copy(
            ytx.at[k, d], yrx.at[k, d], y_send.at[k, d], y_recv.at[k, d],
            device_id={"gy": to}, device_id_type=MESH,
        )

    def store(k):
        t, c = order[k]
        return pltpu.make_async_copy(out_ref.at[t, c], out_hbm.at[t, c], store_sem.at[k])

    def finish(k):
        t, c = order[k]
        out_ref[t, c] = yown[k].reshape(cx, cy, nz)
        for d, receives in ((0, low), (1, high)):

            @pl.when(receives)
            def _(d=d):
                y_copy(k, d, gy).wait_recv()
                out_ref[t, c] += yrx[k, d].astype(jnp.float32).reshape(cx, cy, nz)

        store(k).start()

    for k in range(len(order)):
        acc = own[k]
        if n_gx <= 4:
            for s in range(1, n_gx):
                acc = acc + receive(k, s)
        else:

            acc = lax.fori_loop(1, n_gx, lambda s, acc, k=k: acc + receive(k, s), acc)
        hi, lo = halves(acc)
        wide = jnp.dot(
            jnp.concatenate([hi, lo], axis=0), tmat[...], preferred_element_type=jnp.float32
        )
        zs = 0.5 * acc + (wide[:cells] + wide[cells:]) * inv
        hi, lo = halves(zs)
        v = jnp.dot(
            ymats, jnp.concatenate([hi, lo, hi], axis=0), preferred_element_type=jnp.float32
        )
        yown[k] = v[:cells]
        ytx[k, 0] = v[cells : 2 * cells].astype(jnp.bfloat16)
        ytx[k, 1] = v[2 * cells :].astype(jnp.bfloat16)
        pl.when(high)(y_copy(k, 0, gy + 1).start)
        pl.when(low)(y_copy(k, 1, gy - 1).start)
        if k >= LAG:
            finish(k - LAG)
    for k in range(len(order) - LAG, len(order)):
        finish(k)

    for sends, _, copy, _, _ in exchanges:
        pl.when(sends)(copy.wait_send)
    for k in range(len(order)):
        each(1, n_gx, lambda s, k=k: settle(k, s))
        pl.when(high)(y_copy(k, 0, gy).wait_send)
        pl.when(low)(y_copy(k, 1, gy).wait_send)
        store(k).wait()


def shards(velocity, moved_image, residual_weight, mark_values, mark_brick, mark_cell, band_widths):
    n_gx, n_gy = lax.axis_size("gx"), lax.axis_size("gy")
    steps, cx, cy, nz = moved_image.shape
    rows = mark_values.shape[0]
    cells = cx * cy
    chunks = 3 * steps
    lines = 2 * cells + rows // steps
    f32, bf16 = jnp.float32, jnp.bfloat16
    dma = pltpu.SemaphoreType.DMA
    smoothed = pl.pallas_call(
        functools.partial(kernel, n_gx, n_gy, (steps, cx, cy, nz, rows)),
        out_shape=jax.ShapeDtypeStruct(velocity.shape, f32),
        in_specs=[pl.BlockSpec(memory_space=pltpu.HBM)] * 6,
        out_specs=pl.BlockSpec(memory_space=pltpu.HBM),
        scratch_shapes=[
            pltpu.SMEM(band_widths.shape, jnp.int32),
            pltpu.VMEM(moved_image.shape, f32),
            pltpu.VMEM(residual_weight.shape, f32),
            pltpu.VMEM((3, rows, nz), bf16),
            pltpu.VMEM((1, rows), jnp.int32),
            pltpu.VMEM((1, rows), jnp.int32),
            pltpu.VMEM(velocity.shape, f32),
            dma((8,)),
            dma((chunks,)),
            pltpu.VMEM((chunks, n_gx, cells, nz), jnp.int16),
            pltpu.VMEM((chunks, n_gx, 1, nz), f32),
            pltpu.VMEM((chunks, cells, nz), f32),
            pltpu.VMEM((chunks, n_gx, cells, nz), jnp.int16),
            pltpu.VMEM((chunks, n_gx, 1, nz), f32),
            pltpu.VMEM((chunks, 2, cells, nz), bf16),
            pltpu.VMEM((chunks, cells, nz), f32),
            pltpu.VMEM((chunks, 2, cells, nz), bf16),
            pltpu.VMEM((2, steps, cy, nz), f32),
            pltpu.VMEM((2, steps * cx, nz), f32),
            pltpu.VMEM((2, steps * cx, nz), f32),
            pltpu.VMEM((steps, n_gx * cells, 2 * lines), bf16),
            pltpu.VMEM((nz, nz), bf16),
            dma((chunks, n_gx)),
            dma((chunks, n_gx)),
            dma((chunks, n_gx)),
            dma((chunks, n_gx)),
            dma((chunks, 2)),
            dma((chunks, 2)),
            dma((2,)),
            dma((2,)),
            dma((2,)),
            dma((2,)),
        ],
        compiler_params=pltpu.CompilerParams(
            collective_id=0, has_side_effects=True, vmem_limit_bytes=63 * 2**20
        ),
        cost_estimate=pl.CostEstimate(
            flops=4 * 10**8, bytes_accessed=2 * 10**6, transcendentals=0
        ),
    )(
        band_widths,
        moved_image,
        residual_weight,
        mark_values.transpose(1, 0, 2),
        mark_brick.reshape(1, rows),
        mark_cell.reshape(1, rows),
    )
    return velocity - smoothed


def solution(mesh):
    return jax.shard_map(
        shards,
        mesh=mesh,
        in_specs=(
            P(("group", "ta"), None, "gx", "gy", None),
            P(("group", "ta"), "gx", "gy", None),
            P(("group", "ta"), "gx", "gy", None),
            P(("group", "gx", "gy", "ta"), None, None),
            P(("group", "gx", "gy", "ta"), None),
            P(("group", "gx", "gy", "ta"), None),
            P(),
        ),
        out_specs=P(("group", "ta"), None, "gx", "gy", None),
        check_vma=False,
    )
```

```python
import functools
import math

import jax
import jax.numpy as jnp
from jax import lax
from jax.experimental import pallas as pl
from jax.experimental.pallas import tpu as pltpu
from jax.sharding import PartitionSpec as P

LEVELS = 32000.0
LAG = 2
MESH = pl.DeviceIdType.MESH


def each(start, stop, body):
    if stop - start <= 4:
        for i in range(start, stop):
            body(i)
    else:
        lax.fori_loop(start, stop, lambda i, c: (body(i), c)[1], 0)


def halves(x):
    hi = x.astype(jnp.bfloat16)
    return hi, (x - hi.astype(jnp.float32)).astype(jnp.bfloat16)


def tent(offsets, width):
    w1 = (width + 1).astype(jnp.float32)
    far = jnp.abs(offsets)
    inside = jnp.where(far <= width, (w1 - far.astype(jnp.float32)) / (w1 * w1), 0.0)
    return inside + jnp.where(offsets == 0, 0.5, 0.0)


def kernel(
    n_gx, n_gy, dims, width_hbm, image_hbm, weight_hbm, mark_hbm, brick_hbm, cell_hbm, out_hbm,
    width_ref, image_ref, weight_ref, mark_ref, brick_ref, cell_ref, out_ref, load_sem, store_sem,
    tx, scale_out, own, rx, scale_in, ytx, yown, yrx, edge_x, edge_y_out, edge_y, kmat, tmat,
    tx_send, rx_recv, s_send, s_recv, y_send, y_recv, ex_send, ex_recv, ey_send, ey_recv,
):
    steps, cx, cy, nz, rows = dims
    cells = cx * cy
    per = rows // steps
    lines = 2 * cells + per
    gx, gy = lax.axis_index("gx"), lax.axis_index("gy")
    left, right = gx > 0, gx < n_gx - 1
    low, high = gy > 0, gy < n_gy - 1
    barrier = pltpu.get_barrier_semaphore()

    names = ("width", "brick", "cell", "image", "weight", "mark0", "mark1", "mark2")
    pairs = [(width_hbm, width_ref), (brick_hbm, brick_ref), (cell_hbm, cell_ref)]
    pairs += [(image_hbm, image_ref), (weight_hbm, weight_ref)]
    pairs += [(mark_hbm.at[c], mark_ref.at[c]) for c in range(3)]
    loads = {
        name: pltpu.make_async_copy(src, dst, load_sem.at[i])
        for i, (name, (src, dst)) in enumerate(zip(names, pairs))
    }
    for name in ("image", "width", "brick", "cell", "weight", "mark2", "mark0", "mark1"):
        loads[name].start()

    def greet(s):
        pl.semaphore_signal(
            barrier, inc=1, device_id={"gx": lax.rem(gx + s, n_gx)}, device_id_type=MESH
        )

    each(1, n_gx, greet)

    @pl.when(low)
    def _():
        pl.semaphore_signal(barrier, inc=1, device_id={"gy": gy - 1}, device_id_type=MESH)

    @pl.when(high)
    def _():
        pl.semaphore_signal(barrier, inc=1, device_id={"gy": gy + 1}, device_id_type=MESH)

    def x_edge(d, plane, to):
        return pltpu.make_async_remote_copy(
            image_ref.at[:, plane], edge_x.at[d], ex_send.at[d], ex_recv.at[d],
            device_id={"gx": to}, device_id_type=MESH,
        )

    def y_edge(d, side, to):
        return pltpu.make_async_remote_copy(
            edge_y_out.at[side], edge_y.at[d], ey_send.at[d], ey_recv.at[d],
            device_id={"gy": to}, device_id_type=MESH,
        )

    exchanges = (
        (right, left, x_edge(0, cx - 1, gx + 1), edge_x, 0),
        (left, right, x_edge(1, 0, gx - 1), edge_x, 1),
        (high, low, y_edge(0, 1, gy + 1), edge_y, 0),
        (low, high, y_edge(1, 0, gy - 1), edge_y, 1),
    )
    for name in ("width", "brick", "cell"):
        loads[name].wait()
    group = math.gcd(n_gx, 4)
    block = group * cells
    lane = lax.broadcasted_iota(jnp.int32, (1, lines), 1)
    fcell = lane & (cells - 1)
    for t in range(steps):
        is_mark = (lane >= t * per) & (lane < (t + 1) * per)
        sx = jnp.where(is_mark, brick_ref[...] * cx + cell_ref[...] // cy, gx * cx + fcell // cy)
        sy = jnp.where(is_mark, cell_ref[...] & (cy - 1), fcell & (cy - 1))

        def build(g, t=t, sx=sx, sy=sy):
            r = lax.broadcasted_iota(jnp.int32, (block, lines), 0)
            brick = gx + g * group + r // cells
            brick = jnp.where(brick >= n_gx, brick - n_gx, brick)
            x = brick * cx + (r // cy & (cx - 1))
            k = jnp.where((r & (cy - 1)) == sy, tent(x - sx, width_ref[0]), 0.0)
            hi, lo = halves(k)
            at = pl.ds(pl.multiple_of(g * block, block), block)
            kmat[t, at, 0:lines] = hi
            kmat[t, at, lines : 2 * lines] = lo

        each(0, n_gx // group, build)

    loads["image"].wait()
    for t in range(steps):
        for x in range(cx):
            r = t * cx + x
            edge_y_out[0, r : r + 1, :] = image_ref[t, x, 0:1, :]
            edge_y_out[1, r : r + 1, :] = image_ref[t, x, cy - 1 : cy, :]

    def brick_copy(k, s):
        return pltpu.make_async_remote_copy(
            tx.at[k, s], rx.at[k, s], tx_send.at[k, s], rx_recv.at[k, s],
            device_id={"gx": lax.rem(gx + s, n_gx)}, device_id_type=MESH,
        )

    def scale_copy(k, s):
        return pltpu.make_async_remote_copy(
            scale_out.at[k, s], scale_in.at[k, s], s_send.at[k, s], s_recv.at[k, s],
            device_id={"gx": lax.rem(gx + s, n_gx)}, device_id_type=MESH,
        )

    def send(k, s):
        brick_copy(k, s).start()
        scale_copy(k, s).start()

    def receive(k, s):
        brick_copy(k, s).wait_recv()
        scale_copy(k, s).wait_recv()
        return rx[k, s].astype(jnp.int32).astype(jnp.float32) * jnp.concatenate(
            [scale_in[k, s]] * (nz // 128), axis=1
        )

    def settle(k, s):
        brick_copy(k, s).wait_send()
        scale_copy(k, s).wait_send()

    def meet():
        pl.semaphore_wait(barrier, n_gx - 1 + low.astype(jnp.int32) + high.astype(jnp.int32))

        for sends, receives, copy, buffer, d in exchanges:
            pl.when(sends)(copy.start)

            @pl.when(jnp.logical_not(receives))
            def _(buffer=buffer, d=d):
                buffer[d] = jnp.zeros(buffer.shape[1:], buffer.dtype)

    order = [(t, c) for c in (2, 0, 1) for t in range(steps)]
    for k, (t, c) in enumerate(order):
        if k == steps:
            for _, receives, copy, _, _ in exchanges:
                pl.when(receives)(copy.wait_recv)
        if k == 0:
            loads["weight"].wait()
        if t == 0:
            loads[names[5 + c]].wait()
        m = image_ref[t]
        if c == 2:
            flat = m.reshape(cells, nz)
            z = lax.broadcasted_iota(jnp.int32, (cells, nz), 1)
            after = jnp.where(z == nz - 1, 0.0, pltpu.roll(flat, nz - 1, 1))
            before = jnp.where(z == 0, 0.0, pltpu.roll(flat, 1, 1))
            slope = after - before
        elif c == 0:
            after = jnp.concatenate([m[1:], edge_x[1, t][None]], axis=0)
            before = jnp.concatenate([edge_x[0, t][None], m[:-1]], axis=0)
            slope = (after - before).reshape(cells, nz)
        else:
            flat = m.reshape(cells, nz)
            y = lax.broadcasted_iota(jnp.int32, (cy, nz), 0)
            parts = []
            for x in range(cx):
                r = t * cx + x
                after = jnp.where(y == cy - 1, edge_y[1, r : r + 1, :], pltpu.roll(m[x], cy - 1, 0))
                before = jnp.where(y == 0, edge_y[0, r : r + 1, :], pltpu.roll(m[x], 1, 0))
                parts.append(after - before)
            slope = jnp.concatenate(parts, axis=0)
        hi, lo = halves(weight_ref[t].reshape(cells, nz) * slope * 0.5)
        marks = mark_ref[c, t * per : (t + 1) * per, :]
        pieces = [hi, lo]
        pieces.insert(0 if t == 0 else 2, marks)
        b = jnp.concatenate(pieces, axis=0)
        b = jnp.concatenate([b, b], axis=0)

        def spread(g, k=k, t=t, b=b):
            at = pl.ds(pl.multiple_of(g * block, block), block)
            p = jnp.dot(kmat[t, at, :], b, preferred_element_type=jnp.float32)
            for i in range(group):
                piece = p[i * cells : (i + 1) * cells]
                s = g * group + i
                top = jnp.maximum(jnp.max(jnp.abs(piece), axis=0, keepdims=True), 1e-30)
                top = functools.reduce(jnp.maximum, [top[:, z : z + 128] for z in range(0, nz, 128)])
                fit = jnp.concatenate([LEVELS / top] * (nz // 128), axis=1)
                tx[k, s] = jnp.round(piece * fit).astype(jnp.int32).astype(jnp.int16)
                scale_out[k, s] = top * (1.0 / LEVELS)
                if i == 0:
                    if n_gx == group:
                        own[k] = piece
                    else:

                        @pl.when(g == 0)
                        def _():
                            own[k] = piece

        each(0, n_gx // group, spread)
        if k == steps - 1:
            meet()
        for ready in range(steps) if k == steps - 1 else [k] if k >= steps else []:
            each(1, n_gx, lambda s, k=ready: send(k, s))

    zi = lax.broadcasted_iota(jnp.int32, (nz, nz), 0)
    zj = lax.broadcasted_iota(jnp.int32, (nz, nz), 1)
    tmat[...] = (
        jnp.maximum(width_ref[2] + 1 - jnp.abs(zi - zj), 0).astype(jnp.float32).astype(jnp.bfloat16)
    )
    wz = jnp.full((1, nz), (width_ref[2] + 1).astype(jnp.float32), jnp.float32)
    inv = 1.0 / (wz * wz)

    r = lax.broadcasted_iota(jnp.int32, (3 * cells, cells), 0)
    q = lax.broadcasted_iota(jnp.int32, (3 * cells, cells), 1)
    which = r // cells
    shift = jnp.where(which == 1, cy, jnp.where(which == 2, -cy, 0))
    same = (r // cy & (cx - 1)) == q // cy
    ymat = jnp.where(same, tent((r & (cy - 1)) + shift - (q & (cy - 1)), width_ref[1]), 0.0)
    yhi, ylo = halves(ymat)
    ymats = jnp.concatenate([yhi, yhi, ylo], axis=1)

    def y_copy(k, d, to):
        return pltpu.make_async_remote_copy(
            ytx.at[k, d], yrx.at[k, d], y_send.at[k, d], y_recv.at[k, d],
            device_id={"gy": to}, device_id_type=MESH,
        )

    def store(k):
        t, c = order[k]
        return pltpu.make_async_copy(out_ref.at[t, c], out_hbm.at[t, c], store_sem.at[k])

    def finish(k):
        t, c = order[k]
        out_ref[t, c] = yown[k].reshape(cx, cy, nz)
        for d, receives in ((0, low), (1, high)):

            @pl.when(receives)
            def _(d=d):
                y_copy(k, d, gy).wait_recv()
                out_ref[t, c] += yrx[k, d].astype(jnp.float32).reshape(cx, cy, nz)

        store(k).start()

    for k in range(len(order)):
        acc = own[k]
        if n_gx <= 4:
            for s in range(1, n_gx):
                acc = acc + receive(k, s)
        else:

            acc = lax.fori_loop(1, n_gx, lambda s, acc, k=k: acc + receive(k, s), acc)
        hi, lo = halves(acc)
        wide = jnp.dot(
            jnp.concatenate([hi, lo], axis=0), tmat[...], preferred_element_type=jnp.float32
        )
        zs = 0.5 * acc + (wide[:cells] + wide[cells:]) * inv
        hi, lo = halves(zs)
        v = jnp.dot(
            ymats, jnp.concatenate([hi, lo, hi], axis=0), preferred_element_type=jnp.float32
        )
        yown[k] = v[:cells]
        ytx[k, 0] = v[cells : 2 * cells].astype(jnp.bfloat16)
        ytx[k, 1] = v[2 * cells :].astype(jnp.bfloat16)
        pl.when(high)(y_copy(k, 0, gy + 1).start)
        pl.when(low)(y_copy(k, 1, gy - 1).start)
        if k >= LAG:
            finish(k - LAG)
    for k in range(len(order) - LAG, len(order)):
        finish(k)

    for sends, _, copy, _, _ in exchanges:
        pl.when(sends)(copy.wait_send)
    for k in range(len(order)):
        each(1, n_gx, lambda s, k=k: settle(k, s))
        pl.when(high)(y_copy(k, 0, gy).wait_send)
        pl.when(low)(y_copy(k, 1, gy).wait_send)
        store(k).wait()


def shards(velocity, moved_image, residual_weight, mark_values, mark_brick, mark_cell, band_widths):
    n_gx, n_gy = lax.axis_size("gx"), lax.axis_size("gy")
    steps, cx, cy, nz = moved_image.shape
    rows = mark_values.shape[0]
    cells = cx * cy
    chunks = 3 * steps
    lines = 2 * cells + rows // steps
    f32, bf16 = jnp.float32, jnp.bfloat16
    dma = pltpu.SemaphoreType.DMA
    smoothed = pl.pallas_call(
        functools.partial(kernel, n_gx, n_gy, (steps, cx, cy, nz, rows)),
        out_shape=jax.ShapeDtypeStruct(velocity.shape, f32),
        in_specs=[pl.BlockSpec(memory_space=pltpu.HBM)] * 6,
        out_specs=pl.BlockSpec(memory_space=pltpu.HBM),
        scratch_shapes=[
            pltpu.SMEM(band_widths.shape, jnp.int32),
            pltpu.VMEM(moved_image.shape, f32),
            pltpu.VMEM(residual_weight.shape, f32),
            pltpu.VMEM((3, rows, nz), bf16),
            pltpu.VMEM((1, rows), jnp.int32),
            pltpu.VMEM((1, rows), jnp.int32),
            pltpu.VMEM(velocity.shape, f32),
            dma((8,)),
            dma((chunks,)),
            pltpu.VMEM((chunks, n_gx, cells, nz), jnp.int16),
            pltpu.VMEM((chunks, n_gx, 1, 128), f32),
            pltpu.VMEM((chunks, cells, nz), f32),
            pltpu.VMEM((chunks, n_gx, cells, nz), jnp.int16),
            pltpu.VMEM((chunks, n_gx, 1, 128), f32),
            pltpu.VMEM((chunks, 2, cells, nz), bf16),
            pltpu.VMEM((chunks, cells, nz), f32),
            pltpu.VMEM((chunks, 2, cells, nz), bf16),
            pltpu.VMEM((2, steps, cy, nz), f32),
            pltpu.VMEM((2, steps * cx, nz), f32),
            pltpu.VMEM((2, steps * cx, nz), f32),
            pltpu.VMEM((steps, n_gx * cells, 2 * lines), bf16),
            pltpu.VMEM((nz, nz), bf16),
            dma((chunks, n_gx)),
            dma((chunks, n_gx)),
            dma((chunks, n_gx)),
            dma((chunks, n_gx)),
            dma((chunks, 2)),
            dma((chunks, 2)),
            dma((2,)),
            dma((2,)),
            dma((2,)),
            dma((2,)),
        ],
        compiler_params=pltpu.CompilerParams(
            collective_id=0, has_side_effects=True, vmem_limit_bytes=63 * 2**20
        ),
        cost_estimate=pl.CostEstimate(
            flops=4 * 10**8, bytes_accessed=2 * 10**6, transcendentals=0
        ),
    )(
        band_widths,
        moved_image,
        residual_weight,
        mark_values.transpose(1, 0, 2),
        mark_brick.reshape(1, rows),
        mark_cell.reshape(1, rows),
    )
    return velocity - smoothed


def solution(mesh):
    return jax.shard_map(
        shards,
        mesh=mesh,
        in_specs=(
            P(("group", "ta"), None, "gx", "gy", None),
            P(("group", "ta"), "gx", "gy", None),
            P(("group", "ta"), "gx", "gy", None),
            P(("group", "gx", "gy", "ta"), None, None),
            P(("group", "gx", "gy", "ta"), None),
            P(("group", "gx", "gy", "ta"), None),
            P(),
        ),
        out_specs=P(("group", "ta"), None, "gx", "gy", None),
        check_vma=False,
    )
```
